256 devices in a mesh: row: 4 (over z_hi, core), col: 16 (over z_lo, x), depth: 4 (over y).
Axes of the slice: x: 4, y: 4, z: 8 (z_hi: 2, z_lo: 4; z = z_hi * 4 + z_lo), core: 2. Of those that a mesh axis runs over, the one named last changes fastest.
Arguments:
- tokens: bfloat16 [1536, 6144], P(('depth', 'col'), 'row'), may hold values from -6 to 6
- w_in: bfloat16 [6144, 24576], P('row', 'col'), may hold values from -0.078125 to 0.078125
- w_out: bfloat16 [24576, 6144], P('col', 'row'), may hold values from -0.0390625 to 0.0390625
- grad_out: bfloat16 [1536, 6144], P(('depth', 'col'), 'row'), may hold values from -6 to 6
Outputs:
- layer_out: bfloat16 [1536, 6144], P(('depth', 'col'), 'row')
- grad_tokens: bfloat16 [1536, 6144], P(('depth', 'col'), 'row')
- grad_w_in: bfloat16 [6144, 24576], P(('row', 'depth'), 'col')
- grad_w_out: bfloat16 [24576, 6144], P(('col', 'depth'), 'row')
The draws below stay inside these ranges and needn't reach their ends.
All inputs are finite; a program needn't handle non-finite values.
Results may differ from the reference program's by a relative error of at most 0.0049.
Values may be sent and summed in bfloat16 or wider, within the bound.
No kernel may reach another device: no remote copies, remote signals or barrier semaphores. Data moves between devices by JAX's collectives and lax.ppermute only.
A program may use at most 128 MiB of HBM per device.

```python
import jax
import jax.numpy as jnp
from jax import lax

D = 6144
FF = 24576
TOKENS = 1536


def shard_levels(own_key, shape, pieces, low, largest):
    level = 1.0
    for dim, parts in pieces:
        draws = jax.random.uniform(jax.random.fold_in(jax.random.fold_in(own_key, 6), dim), (parts,), jnp.float32, low / len(pieces), largest / len(pieces))
        level = level * jnp.repeat(jnp.exp(draws), shape[dim] // parts).reshape((-1,) + (1,) * (len(shape) - 1 - dim))
    return level


def noise(rng, dims, deviation, bound, split=(), held_as=jnp.bfloat16):
    values = deviation * jax.random.normal(rng, dims, jnp.float32)
    if split:
        values = values * shard_levels(rng, dims, split, -0.22, 0.18)
    return jnp.clip(values, -bound, bound).astype(held_as)


def setup_inputs(seed: int = 0) -> dict:
    splits = jax.random.split(jax.random.key(seed), 5)
    tokens = noise(splits[0], (TOKENS, D), 1.0, 6.0, ((0, 64), (1, 4)))
    w_in = noise(splits[1], (D, FF), D ** -0.5, 0.078125, ((0, 4), (1, 16)))
    w_out = noise(splits[2], (FF, D), FF ** -0.5, 0.0390625, ((0, 16), (1, 4)))
    grad_out = noise(splits[3], (TOKENS, D), 1.0, 6.0, ((0, 64), (1, 4)))
    return dict(tokens=tokens, w_in=w_in, w_out=w_out, grad_out=grad_out)


coef = 0.7978845608


def gelu_pair(z):
    t = jnp.tanh(coef * (z + 0.044715 * z * z * z))
    value = 0.5 * z * (1.0 + t)
    slope = 0.5 * (1.0 + t) + 0.5 * z * (1.0 - t * t) * coef * (1.0 + 0.134145 * z * z)
    return value, slope


def reference(tokens, w_in, w_out, grad_out):
    pre = jnp.dot(tokens, w_in, preferred_element_type=jnp.float32)
    value, slope = gelu_pair(pre)
    act = value.astype(jnp.bfloat16)
    layer_out = jnp.dot(act, w_out, preferred_element_type=jnp.float32).astype(jnp.bfloat16)
    grad_act = lax.dot_general(grad_out, w_out, (((1,), (1,)), ((), ())), preferred_element_type=jnp.float32)
    grad_pre = (grad_act * slope).astype(jnp.bfloat16)
    grad_tokens = lax.dot_general(grad_pre, w_in, (((1,), (1,)), ((), ())), preferred_element_type=jnp.float32).astype(jnp.bfloat16)
    grad_w_in = lax.dot_general(tokens, grad_pre, (((0,), (0,)), ((), ())), preferred_element_type=jnp.float32).astype(jnp.bfloat16)
    grad_w_out = lax.dot_general(act, grad_out, (((0,), (0,)), ((), ())), preferred_element_type=jnp.float32).astype(jnp.bfloat16)
    return layer_out, grad_tokens, grad_w_in, grad_w_out
```

```python
import jax
import jax.numpy as jnp
from jax import lax
from jax.sharding import PartitionSpec as P

coef = 0.7978845608
AXES = ("row", "col", "depth")
BF = jnp.bfloat16
F32 = jnp.float32


def gelu_pair(z):
    t = jnp.tanh(coef * (z + 0.044715 * z * z * z))
    value = 0.5 * z * (1.0 + t)
    slope = 0.5 * (1.0 + t) + 0.5 * z * (1.0 - t * t) * coef * (1.0 + 0.134145 * z * z)
    return (value, slope)


def dot(left, right, dims):
    return lax.dot_general(left, right, ((dims[:1], dims[1:]), ((), ())), preferred_element_type=F32)


def send(array, hi=0, core=0, lo=0, x=0, y=0):
    pairs = []
    for z_hi in range(2):
        for c in range(2):
            for z_lo in range(4):
                for i in range(4):
                    for j in range(4):
                        here = ((z_hi * 2 + c) * 16 + z_lo * 4 + i) * 4 + j
                        there = (
                            ((z_hi + hi) % 2 * 2 + (c + core) % 2) * 16 + (z_lo + lo) % 4 * 4 + (i + x) % 4
                        ) * 4 + (j + y) % 4
                        pairs.append((here, there))
    return lax.ppermute(array, AXES, pairs)


def gather_lo(shard):
    return jnp.concatenate([shard] + [send(shard, lo=-k) for k in (1, 2, 3)], axis=0)


def gather_x(part):
    return jnp.concatenate([part] + [send(part, x=-k) for k in (1, 2, 3)], axis=0)


def scatter_col(part):
    blocks = part.reshape(4, 96, 1536)
    total = blocks[0]
    arrived = [send(blocks[k].astype(BF), x=k) for k in (1, 2, 3)]
    for block in arrived:
        total = total + block.astype(F32)
    blocks = total.reshape(4, 24, 1536)
    total = blocks[0]
    arrived = [send(blocks[k].astype(BF), lo=k) for k in (1, 2, 3)]
    for block in arrived:
        total = total + block.astype(F32)
    return total.astype(BF)


def sum_row(mine, other):
    total = mine + send(other, core=1).astype(F32)
    rounded = total.astype(BF)
    half = rounded.shape[0] // 2
    arrived = jnp.concatenate([send(rounded[:half], hi=1), send(rounded[half:], hi=1)], axis=0)
    return total + arrived.astype(F32)


def local(tokens, w_in, w_out, grad_out):
    core = lax.axis_index("row") % 2
    y = lax.axis_index("depth")
    w_in_mine = lax.dynamic_slice_in_dim(w_in, core * 768, 768, axis=1)
    w_in_other = lax.dynamic_slice_in_dim(w_in, (1 - core) * 768, 768, axis=1)
    w_out_mine = lax.dynamic_slice_in_dim(w_out, core * 768, 768, axis=0)
    w_out_other = lax.dynamic_slice_in_dim(w_out, (1 - core) * 768, 768, axis=0)

    token_part = gather_lo(tokens)
    cot_part = gather_lo(grad_out)
    token_rows = gather_x(token_part)
    cot_rows = gather_x(cot_part)

    pre_other = dot(token_rows, w_in_other, (1, 0)).astype(BF)
    pre_mine = dot(token_rows, w_in_mine, (1, 0))
    pre = sum_row(pre_mine, pre_other)

    def token_cols(k):
        return lax.dynamic_slice_in_dim(token_rows, (y + k) % 4 * 384, 384, axis=1)

    token_all = jnp.concatenate([token_cols(0)] + [send(token_cols(k), y=k) for k in (1, 2, 3)], axis=0)

    grad_other = dot(cot_rows, w_out_other, (1, 1)).astype(BF)
    grad_mine = dot(cot_rows, w_out_mine, (1, 1))
    grad_act = sum_row(grad_mine, grad_other)

    below = send(cot_rows, y=1)
    above = send(cot_rows, y=-1)
    far = jnp.concatenate([send(below[:192], y=1), send(above[192:], y=-1)], axis=0)
    cot_all = jnp.concatenate([cot_rows, below, far, above], axis=0)

    value, slope = gelu_pair(pre)
    act_mine = value.astype(BF)
    act_other = send(act_mine, core=1)
    out_part = dot(act_mine, w_out_mine, (1, 0)) + dot(act_other, w_out_other, (1, 0))
    layer_out = scatter_col(out_part)

    act_rows = jnp.concatenate([act_mine, act_other], axis=1)

    def act_cols(k):
        return lax.dynamic_slice_in_dim(act_rows, (y + k + 2 * core) % 4 * 384, 384, axis=1)

    act_all = jnp.concatenate([act_cols(0)] + [send(act_cols(k), y=k) for k in (1, 2, 3)], axis=0)
    grad_w_out = dot(act_all, cot_all, (0, 0)).astype(BF)

    grad_pre_mine = (grad_act * slope).astype(BF)
    grad_pre_other = send(grad_pre_mine, core=1)
    in_part = dot(grad_pre_mine, w_in_mine, (1, 1)) + dot(grad_pre_other, w_in_other, (1, 1))
    grad_tokens = scatter_col(in_part)

    far_mine = jnp.concatenate([send(grad_pre_mine, y=k) for k in (1, 2, 3)], axis=0)
    far_other = send(far_mine, core=1)
    all_mine = jnp.concatenate([grad_pre_mine, far_mine], axis=0)
    all_other = jnp.concatenate([grad_pre_other, far_other], axis=0)
    first_mine = dot(token_all, all_mine, (0, 0)).astype(BF)
    first_other = dot(token_all, all_other, (0, 0)).astype(BF)
    grad_w_in = jnp.concatenate(
        [jnp.where(core == 0, first_mine, first_other), jnp.where(core == 0, first_other, first_mine)], axis=1
    )
    return (layer_out, grad_tokens, grad_w_in, grad_w_out)


def solution(mesh):
    return jax.shard_map(
        local,
        mesh=mesh,
        in_specs=(
            P(("depth", "col"), "row"),
            P("row", "col"),
            P("col", "row"),
            P(("depth", "col"), "row"),
        ),
        out_specs=(
            P(("depth", "col"), "row"),
            P(("depth", "col"), "row"),
            P(("row", "depth"), "col"),
            P(("col", "depth"), "row"),
        ),
        check_vma=False,
    )
```

```python
import jax
import jax.numpy as jnp
from jax import lax
from jax.sharding import PartitionSpec as P

coef = 0.7978845608
AXES = ("row", "col", "depth")
BF = jnp.bfloat16
F32 = jnp.float32


def gelu_pair(z):
    t = jnp.tanh(coef * (z + 0.044715 * z * z * z))
    value = 0.5 * z * (1.0 + t)
    slope = 0.5 * (1.0 + t) + 0.5 * z * (1.0 - t * t) * coef * (1.0 + 0.134145 * z * z)
    return (value, slope)


def dot(left, right, dims):
    return lax.dot_general(left, right, ((dims[:1], dims[1:]), ((), ())), preferred_element_type=F32)


def send(array, hi=0, core=0, lo=0, x=0, y=0):
    pairs = []
    for z_hi in range(2):
        for c in range(2):
            for z_lo in range(4):
                for i in range(4):
                    for j in range(4):
                        here = ((z_hi * 2 + c) * 16 + z_lo * 4 + i) * 4 + j
                        there = (
                            ((z_hi + hi) % 2 * 2 + (c + core) % 2) * 16 + (z_lo + lo) % 4 * 4 + (i + x) % 4
                        ) * 4 + (j + y) % 4
                        pairs.append((here, there))
    return lax.ppermute(array, AXES, pairs)


def exchange(array, turn):
    pairs = []
    for row in range(4):
        flip = 1 if row % 2 == turn else 3
        for col in range(16):
            for y in range(4):
                pairs.append(((row * 16 + col) * 4 + y, (row * 16 + col) * 4 + (y ^ flip)))
    return lax.ppermute(array, AXES, pairs)


def after(array, *others):
    return lax.optimization_barrier((array, *others))[0]


def front(token_block, cot_block, weights):
    in_mine, in_other, out_mine, out_other = weights
    other = jnp.stack([dot(token_block, in_other, (1, 0)).astype(BF), dot(cot_block, out_other, (1, 1)).astype(BF)])
    mine = jnp.stack([dot(token_block, in_mine, (1, 0)), dot(cot_block, out_mine, (1, 1))])
    return mine + send(other, core=1).astype(F32)


def cross(total):
    payload = total.astype(BF)
    return payload, send(payload, hi=1)


def middle(total, arrived):
    both = total + arrived.astype(F32)
    value, slope = gelu_pair(both[0])
    return jnp.stack([value.astype(BF), (both[1] * slope).astype(BF)])


def back(mine, other, weights):
    in_mine, in_other, out_mine, out_other = weights
    return jnp.stack(
        [
            dot(mine[0], out_mine, (1, 0)) + dot(other[0], out_other, (1, 0)),
            dot(mine[1], in_mine, (1, 1)) + dot(other[1], in_other, (1, 1)),
        ]
    )


def local(tokens, w_in, w_out, grad_out):
    core = lax.axis_index("row") % 2
    y = lax.axis_index("depth")
    weights = lax.optimization_barrier(
        (
            lax.dynamic_slice_in_dim(w_in, core * 768, 768, axis=1),
            lax.dynamic_slice_in_dim(w_in, (1 - core) * 768, 768, axis=1),
            lax.dynamic_slice_in_dim(w_out, core * 768, 768, axis=0),
            lax.dynamic_slice_in_dim(w_out, (1 - core) * 768, 768, axis=0),
        )
    )
    first = y ^ (1 + 2 * core)
    second = y ^ (3 - 2 * core)

    own = jnp.stack([tokens, grad_out])
    block0 = jnp.concatenate([own] + [send(own, lo=-k) for k in (1, 2, 3)], axis=1)
    block1 = send(block0, x=-1)
    block3 = send(block0, x=-3)
    near = jnp.concatenate([block1, block3], axis=1)
    total0 = front(block0[0], block0[1], weights)
    payload0, arrived0 = cross(total0)
    block2 = send(after(block0, near), x=-2)
    total1 = front(near[0], near[1], weights)
    payload1, arrived1 = cross(total1)
    block2 = after(block2, payload1)
    total2 = front(block2[0], block2[1], weights)
    payload2, arrived2 = cross(total2)

    def split(rows, shift):
        def quarter(q):
            return lax.dynamic_slice_in_dim(rows, (q + shift) % 4 * 384, 384, axis=1)

        return quarter(y), quarter(second), jnp.concatenate([quarter(first), quarter(y ^ 2)], axis=1)

    def pair_rows(mine, other):
        own, second_part, out = split(jnp.concatenate([mine[0], other[0]], axis=1), 2 * core)
        low = jnp.where(core == 0, mine[1], other[1])
        high = jnp.where(core == 0, other[1], mine[1])
        grad = jnp.concatenate([low, high], axis=1)
        far = exchange(jnp.concatenate([out, grad], axis=1), 0)
        return own, second_part, grad, far

    token0 = split(jnp.concatenate([block0[0], near[0]], axis=0), 0)
    cot0 = jnp.concatenate([block0[1], near[1]], axis=0)
    far0 = exchange(after(jnp.concatenate([cot0, token0[2]], axis=1), payload1), 0)
    token1 = split(block2[0], 0)
    far1 = exchange(after(jnp.concatenate([block2[1], token1[2]], axis=1), payload2), 0)

    mine0 = middle(total0, after(arrived0, payload1))
    other0 = send(mine0, core=1)
    pair0 = pair_rows(mine0, other0)

    mine1 = middle(total1, arrived1)
    other1 = send(mine1, core=1)
    pair1 = pair_rows(after(mine1, far0), other1)
    mine2 = middle(total2, after(arrived2, other1, pair1[3]))
    other2 = send(mine2, core=1)
    pair2 = pair_rows(after(mine2, pair0[3], far1), other2)

    cot_pair = jnp.concatenate([cot0, block2[1], far0[:, :1536], far1[:, :1536]], axis=0)
    token_own = jnp.concatenate([token0[0], token1[0], far0[:, 1536:1920], far1[:, 1536:1920]], axis=0)
    token_second = jnp.concatenate([token0[1], token1[1], far0[:, 1920:], far1[:, 1920:]], axis=0)
    cot_pair, token_own, token_second = lax.optimization_barrier((cot_pair, token_own, token_second))

    pairs = (pair0, pair1, pair2)

    def joined(i, cols):
        return jnp.concatenate([p[i] for p in pairs] + [p[3][:, cols] for p in pairs], axis=0)

    act_own = joined(0, slice(0, 384))
    act_second = joined(1, slice(384, 768))
    grad_pair = joined(2, slice(768, 2304))
    act_own, act_second, grad_pair = lax.optimization_barrier((act_own, act_second, grad_pair))
    out_sent = dot(act_second, cot_pair, (0, 0)).astype(BF)
    in_sent = dot(token_second, grad_pair, (0, 0)).astype(BF)
    out_kept, in_kept = lax.optimization_barrier(
        (dot(act_own, cot_pair, (0, 0)), dot(token_own, grad_pair, (0, 0)))
    )
    grad_w_out = (out_kept + exchange(out_sent, 1).astype(F32)).astype(BF)
    grad_w_in = (in_kept + exchange(in_sent, 1).astype(F32)).astype(BF)

    result0 = back(after(mine0, mine2), other0, weights)
    result1 = back(mine1, other1, weights).astype(BF)
    result2 = back(mine2, other2, weights).astype(BF)
    got1 = send(result1[:, :96], x=1)
    got3 = send(result1[:, 96:], x=3)
    got2 = send(result2, x=2)
    total = result0 + got1.astype(F32) + got3.astype(F32) + got2.astype(F32)
    total = after(total, out_sent, in_sent)
    sums = total[:, :24]
    for k in (1, 2, 3):
        sums = sums + send(total[:, 24 * k : 24 * k + 24].astype(BF), lo=k).astype(F32)
    layer_out = sums[0].astype(BF)
    grad_tokens = sums[1].astype(BF)

    return (layer_out, grad_tokens, grad_w_in, grad_w_out)


def solution(mesh):
    return jax.shard_map(
        local,
        mesh=mesh,
        in_specs=(
            P(("depth", "col"), "row"),
            P("row", "col"),
            P("col", "row"),
            P(("depth", "col"), "row"),
        ),
        out_specs=(
            P(("depth", "col"), "row"),
            P(("depth", "col"), "row"),
            P(("row", "depth"), "col"),
            P(("col", "depth"), "row"),
        ),
        check_vma=False,
    )
```

```python
import jax
import jax.numpy as jnp
from jax import lax
from jax.sharding import PartitionSpec as P

coef = 0.7978845608
AXES = ("row", "col", "depth")
BF = jnp.bfloat16
F32 = jnp.float32


def gelu_pair(z):
    t = jnp.tanh(coef * (z + 0.044715 * z * z * z))
    value = 0.5 * z * (1.0 + t)
    slope = 0.5 * (1.0 + t) + 0.5 * z * (1.0 - t * t) * coef * (1.0 + 0.134145 * z * z)
    return (value, slope)


def dot(left, right, dims):
    return lax.dot_general(left, right, ((dims[:1], dims[1:]), ((), ())), preferred_element_type=F32)


def send(array, hi=0, core=0, lo=0, x=0, y=0):
    pairs = []
    for z_hi in range(2):
        for c in range(2):
            for z_lo in range(4):
                for i in range(4):
                    for j in range(4):
                        here = ((z_hi * 2 + c) * 16 + z_lo * 4 + i) * 4 + j
                        there = (
                            ((z_hi + hi) % 2 * 2 + (c + core) % 2) * 16 + (z_lo + lo) % 4 * 4 + (i + x) % 4
                        ) * 4 + (j + y) % 4
                        pairs.append((here, there))
    return lax.ppermute(array, AXES, pairs)


def exchange(array, turn):
    pairs = []
    for row in range(4):
        flip = 1 if row % 2 == turn else 3
        for col in range(16):
            for y in range(4):
                pairs.append(((row * 16 + col) * 4 + y, (row * 16 + col) * 4 + (y ^ flip)))
    return lax.ppermute(array, AXES, pairs)


def after(array, *others):
    return lax.optimization_barrier((array, *others))[0]


def front(token_block, cot_block, weights):
    in_mine, in_other, out_mine, out_other = weights
    other = jnp.stack([dot(token_block, in_other, (1, 0)).astype(BF), dot(cot_block, out_other, (1, 1)).astype(BF)])
    mine = jnp.stack([dot(token_block, in_mine, (1, 0)), dot(cot_block, out_mine, (1, 1))])
    return mine + send(other, core=1).astype(F32)


def cross(total):
    payload = total.astype(BF)
    return payload, send(payload, hi=1)


def middle(total, arrived):
    both = total + arrived.astype(F32)
    value, slope = gelu_pair(both[0])
    return jnp.stack([value.astype(BF), (both[1] * slope).astype(BF)])


def back(mine, other, weights):
    in_mine, in_other, out_mine, out_other = weights
    return jnp.stack(
        [
            dot(mine[0], out_mine, (1, 0)) + dot(other[0], out_other, (1, 0)),
            dot(mine[1], in_mine, (1, 1)) + dot(other[1], in_other, (1, 1)),
        ]
    )


def local(tokens, w_in, w_out, grad_out):
    core = lax.axis_index("row") % 2
    y = lax.axis_index("depth")
    weights = lax.optimization_barrier(
        (
            lax.dynamic_slice_in_dim(w_in, core * 768, 768, axis=1),
            lax.dynamic_slice_in_dim(w_in, (1 - core) * 768, 768, axis=1),
            lax.dynamic_slice_in_dim(w_out, core * 768, 768, axis=0),
            lax.dynamic_slice_in_dim(w_out, (1 - core) * 768, 768, axis=0),
        )
    )
    first = y ^ (1 + 2 * core)
    second = y ^ (3 - 2 * core)

    own = jnp.stack([tokens, grad_out])
    block0 = jnp.concatenate([own] + [send(own, lo=-k) for k in (1, 2, 3)], axis=1)
    block1 = send(block0, x=-1)
    block3 = send(block0, x=-3)
    near = jnp.concatenate([block1, block3], axis=1)
    total0 = front(block0[0], block0[1], weights)
    payload0, arrived0 = cross(total0)
    block2 = jnp.stack([send(block1[0], x=-1), send(block3[1], x=1)])
    total1 = front(near[0], near[1], weights)
    payload1, arrived1 = cross(total1)
    block2 = after(block2, payload1)
    total2 = front(block2[0], block2[1], weights)
    payload2, arrived2 = cross(total2)

    def split(rows, shift):
        def quarter(q):
            return lax.dynamic_slice_in_dim(rows, (q + shift) % 4 * 384, 384, axis=1)

        return quarter(y), quarter(second), jnp.concatenate([quarter(first), quarter(y ^ 2)], axis=1)

    def pair_rows(mine, other):
        own, second_part, out = split(jnp.concatenate([mine[0], other[0]], axis=1), 2 * core)
        low = jnp.where(core == 0, mine[1], other[1])
        high = jnp.where(core == 0, other[1], mine[1])
        grad = jnp.concatenate([low, high], axis=1)
        return own, second_part, grad, jnp.concatenate([out, grad], axis=1)

    token0 = split(jnp.concatenate([block0[0], near[0]], axis=0), 0)
    cot0 = jnp.concatenate([block0[1], near[1]], axis=0)
    far0 = exchange(after(jnp.concatenate([cot0, token0[2]], axis=1), payload1), 0)
    token1 = split(block2[0], 0)

    mine0 = middle(total0, after(arrived0, payload1))
    other0 = send(mine0, core=1)
    pair0 = pair_rows(mine0, other0)
    far1 = exchange(jnp.concatenate([block2[1], token1[2], pair0[3]], axis=1), 0)

    mine1 = middle(total1, after(arrived1, far0))
    other1 = send(mine1, core=1)
    pair1 = pair_rows(mine1, other1)
    got1 = exchange(pair1[3], 0)
    result1 = back(after(mine1, pair1[3]), other1, weights).astype(BF)
    mine2 = middle(total2, after(arrived2, pair1[3]))
    other2 = send(after(mine2, result1), core=1)
    pair2 = pair_rows(after(mine2, far1, far0), other2)
    got2 = exchange(pair2[3], 0)

    cot_pair = jnp.concatenate([cot0, block2[1], far0[:, :1536], far1[:, :1536]], axis=0)
    token_own = jnp.concatenate([token0[0], token1[0], far0[:, 1536:1920], far1[:, 1536:1920]], axis=0)
    token_second = jnp.concatenate([token0[1], token1[1], far0[:, 1920:], far1[:, 1920:2304]], axis=0)
    cot_pair, token_own, token_second = lax.optimization_barrier((cot_pair, token_own, token_second))

    pairs = (pair0, pair1, pair2)
    gots = (far1[:, 2304:], got1, got2)

    def joined(i, cols):
        return jnp.concatenate([p[i] for p in pairs] + [p[:, cols] for p in gots], axis=0)

    act_own = joined(0, slice(0, 384))
    act_second = joined(1, slice(384, 768))
    grad_pair = joined(2, slice(768, 2304))
    act_own, act_second, grad_pair = lax.optimization_barrier((act_own, act_second, grad_pair))
    out_sent = dot(act_second, cot_pair, (0, 0)).astype(BF)
    out_kept, in_kept = lax.optimization_barrier(
        (dot(act_own, cot_pair, (0, 0)), dot(token_own, grad_pair, (0, 0)))
    )
    in_sent = dot(after(token_second, out_kept, in_kept), grad_pair, (0, 0)).astype(BF)
    grad_w_out = (out_kept + exchange(out_sent, 1).astype(F32)).astype(BF)
    grad_w_in = (in_kept + exchange(in_sent, 1).astype(F32)).astype(BF)

    result0 = back(after(mine0, pair2[3]), other0, weights)
    result2 = back(after(mine2, pair2[3]), other2, weights).astype(BF)
    total = result0
    for part in (send(result1[:, :96], x=1), send(result1[:, 96:], x=3), send(result2, x=2)):
        total = total + part.astype(F32)
    total = after(total, out_sent, in_sent)
    arrived = [send(total[:, 24 * k : 24 * k + 24].astype(BF), lo=k) for k in (1, 2, 3)]

    sums = total[:, :24]
    for part in arrived:
        sums = sums + after(part, grad_w_out, grad_w_in).astype(F32)
    layer_out = sums[0].astype(BF)
    grad_tokens = sums[1].astype(BF)
    return (layer_out, grad_tokens, grad_w_in, grad_w_out)


def solution(mesh):
    return jax.shard_map(
        local,
        mesh=mesh,
        in_specs=(
            P(("depth", "col"), "row"),
            P("row", "col"),
            P("col", "row"),
            P(("depth", "col"), "row"),
        ),
        out_specs=(
            P(("depth", "col"), "row"),
            P(("depth", "col"), "row"),
            P(("row", "depth"), "col"),
            P(("col", "depth"), "row"),
        ),
        check_vma=False,
    )
```

```python
import jax
import jax.numpy as jnp
from jax import lax
from jax.sharding import PartitionSpec as P

coef = 0.7978845608
AXES = ("row", "col", "depth")
BF = jnp.bfloat16
F32 = jnp.float32


def gelu_pair(z):
    t = jnp.tanh(coef * (z + 0.044715 * z * z * z))
    value = 0.5 * z * (1.0 + t)
    slope = 0.5 * (1.0 + t) + 0.5 * z * (1.0 - t * t) * coef * (1.0 + 0.134145 * z * z)
    return (value, slope)


def dot(left, right, dims):
    return lax.dot_general(left, right, ((dims[:1], dims[1:]), ((), ())), preferred_element_type=F32)


def send(array, hi=0, core=0, lo=0, x=0, y=0):
    pairs = []
    for z_hi in range(2):
        for c in range(2):
            for z_lo in range(4):
                for i in range(4):
                    for j in range(4):
                        here = ((z_hi * 2 + c) * 16 + z_lo * 4 + i) * 4 + j
                        there = (
                            ((z_hi + hi) % 2 * 2 + (c + core) % 2) * 16 + (z_lo + lo) % 4 * 4 + (i + x) % 4
                        ) * 4 + (j + y) % 4
                        pairs.append((here, there))
    return lax.ppermute(array, AXES, pairs)


def exchange(array, turn):
    pairs = []
    for row in range(4):
        flip = 1 if row % 2 == turn else 3
        for col in range(16):
            for y in range(4):
                pairs.append(((row * 16 + col) * 4 + y, (row * 16 + col) * 4 + (y ^ flip)))
    return lax.ppermute(array, AXES, pairs)


def after(array, *others):
    return lax.optimization_barrier((array, *others))[0]


def front(token_block, cot_block, weights):
    in_mine, in_other, out_mine, out_other = weights
    other = jnp.stack([dot(token_block, in_other, (1, 0)).astype(BF), dot(cot_block, out_other, (1, 1)).astype(BF)])
    mine = jnp.stack([dot(token_block, in_mine, (1, 0)), dot(cot_block, out_mine, (1, 1))])
    return mine + send(other, core=1).astype(F32)


def cross(total):
    payload = total.astype(BF)
    return payload, send(payload, hi=1)


def middle(total, arrived):
    both = total + arrived.astype(F32)
    value, slope = gelu_pair(both[0])
    return jnp.stack([value.astype(BF), (both[1] * slope).astype(BF)])


def back(mine, other, weights):
    in_mine, in_other, out_mine, out_other = weights
    return jnp.stack(
        [
            dot(mine[0], out_mine, (1, 0)) + dot(other[0], out_other, (1, 0)),
            dot(mine[1], in_mine, (1, 1)) + dot(other[1], in_other, (1, 1)),
        ]
    )


def local(tokens, w_in, w_out, grad_out):
    core = lax.axis_index("row") % 2
    y = lax.axis_index("depth")
    weights = lax.optimization_barrier(
        (
            lax.dynamic_slice_in_dim(w_in, core * 768, 768, axis=1),
            lax.dynamic_slice_in_dim(w_in, (1 - core) * 768, 768, axis=1),
            lax.dynamic_slice_in_dim(w_out, core * 768, 768, axis=0),
            lax.dynamic_slice_in_dim(w_out, (1 - core) * 768, 768, axis=0),
        )
    )
    first = y ^ (1 + 2 * core)
    second = y ^ (3 - 2 * core)

    own = jnp.stack([tokens, grad_out])
    block0 = jnp.concatenate([own] + [send(own, lo=-k) for k in (1, 2, 3)], axis=1)
    block1 = send(block0, x=-1)
    block3 = send(block0, x=-3)
    near = jnp.concatenate([block1, block3], axis=1)
    total0 = front(block0[0], block0[1], weights)
    payload0, arrived0 = cross(total0)
    total1 = front(near[0], near[1], weights)
    payload1, arrived1 = cross(total1)
    block1, block3 = after(block1, payload1), after(block3, payload1)
    block2 = jnp.stack([send(block1[0], x=-1), send(block3[1], x=1)])
    total2 = front(block2[0], block2[1], weights)
    payload2, arrived2 = cross(total2)

    def split(rows, shift):
        def quarter(q):
            return lax.dynamic_slice_in_dim(rows, (q + shift) % 4 * 384, 384, axis=1)

        return quarter(y), quarter(second), jnp.concatenate([quarter(first), quarter(y ^ 2)], axis=1)

    def pair_rows(mine, other):
        own, second_part, out = split(jnp.concatenate([mine[0], other[0]], axis=1), 2 * core)
        low = jnp.where(core == 0, mine[1], other[1])
        high = jnp.where(core == 0, other[1], mine[1])
        grad = jnp.concatenate([low, high], axis=1)
        return own, second_part, grad, jnp.concatenate([out, grad], axis=1)

    token0 = split(jnp.concatenate([block0[0], near[0]], axis=0), 0)
    cot0 = jnp.concatenate([block0[1], near[1]], axis=0)
    far0 = exchange(after(jnp.concatenate([cot0, token0[2]], axis=1), payload1), 0)
    token1 = split(block2[0], 0)

    mine0 = middle(total0, after(arrived0, payload2))
    other0 = send(mine0, core=1)
    pair0 = pair_rows(mine0, other0)
    far1 = exchange(jnp.concatenate([block2[1], token1[2], pair0[3]], axis=1), 0)

    mine1 = middle(total1, after(arrived1, far0))
    other1 = send(mine1, core=1)
    pair1 = pair_rows(mine1, other1)
    got1 = exchange(pair1[3], 0)
    result1 = back(after(mine1, pair1[3]), other1, weights).astype(BF)
    mine2 = middle(total2, after(arrived2, pair1[3]))
    other2 = send(after(mine2, result1), core=1)
    pair2 = pair_rows(after(mine2, far1, far0), other2)
    got2 = exchange(pair2[3], 0)

    cot_pair = jnp.concatenate([cot0, block2[1], far0[:, :1536], far1[:, :1536]], axis=0)
    token_own = jnp.concatenate([token0[0], token1[0], far0[:, 1536:1920], far1[:, 1536:1920]], axis=0)
    token_second = jnp.concatenate([token0[1], token1[1], far0[:, 1920:], far1[:, 1920:2304]], axis=0)
    cot_pair, token_own, token_second = lax.optimization_barrier((cot_pair, token_own, token_second))

    pairs = (pair0, pair1, pair2)
    gots = (far1[:, 2304:], got1, got2)

    def joined(i, cols):
        return jnp.concatenate([p[i] for p in pairs] + [p[:, cols] for p in gots], axis=0)

    act_own = joined(0, slice(0, 384))
    act_second = joined(1, slice(384, 768))
    grad_pair = joined(2, slice(768, 2304))
    act_own, act_second, grad_pair = lax.optimization_barrier((act_own, act_second, grad_pair))
    out_sent = dot(act_second, cot_pair, (0, 0)).astype(BF)
    out_kept, in_kept = lax.optimization_barrier(
        (dot(act_own, cot_pair, (0, 0)), dot(token_own, grad_pair, (0, 0)))
    )
    in_sent = dot(after(token_second, out_kept, in_kept), grad_pair, (0, 0)).astype(BF)
    grad_w_out = (out_kept + exchange(out_sent, 1).astype(F32)).astype(BF)
    grad_w_in = (in_kept + exchange(in_sent, 1).astype(F32)).astype(BF)

    result0 = back(after(mine0, pair2[3]), other0, weights)
    result2 = back(after(mine2, pair2[3]), other2, weights).astype(BF)
    total = result0
    for part in (send(result1[:, :96], x=1), send(result1[:, 96:], x=3), send(result2, x=2)):
        total = total + part.astype(F32)
    total = after(total, out_sent, in_sent)
    arrived = [send(total[:, 24 * k : 24 * k + 24].astype(BF), lo=k) for k in (1, 2, 3)]

    sums = total[:, :24]
    for part in arrived:
        sums = sums + after(part, grad_w_out, grad_w_in).astype(F32)
    layer_out = sums[0].astype(BF)
    grad_tokens = sums[1].astype(BF)
    return (layer_out, grad_tokens, grad_w_in, grad_w_out)


def solution(mesh):
    return jax.shard_map(
        local,
        mesh=mesh,
        in_specs=(
            P(("depth", "col"), "row"),
            P("row", "col"),
            P("col", "row"),
            P(("depth", "col"), "row"),
        ),
        out_specs=(
            P(("depth", "col"), "row"),
            P(("depth", "col"), "row"),
            P(("row", "depth"), "col"),
            P(("col", "depth"), "row"),
        ),
        check_vma=False,
    )
```

```python
import jax
import jax.numpy as jnp
from jax import lax
from jax.sharding import PartitionSpec as P

coef = 0.7978845608
AXES = ("row", "col", "depth")
BF = jnp.bfloat16
F32 = jnp.float32


def gelu_pair(z):
    t = jnp.tanh(coef * (z + 0.044715 * z * z * z))
    value = 0.5 * z * (1.0 + t)
    slope = 0.5 * (1.0 + t) + 0.5 * z * (1.0 - t * t) * coef * (1.0 + 0.134145 * z * z)
    return (value, slope)


def dot(left, right, dims):
    return lax.dot_general(left, right, ((dims[:1], dims[1:]), ((), ())), preferred_element_type=F32)


def send(array, hi=0, core=0, lo=0, x=0, y=0):
    pairs = []
    for z_hi in range(2):
        for c in range(2):
            for z_lo in range(4):
                for i in range(4):
                    for j in range(4):
                        here = ((z_hi * 2 + c) * 16 + z_lo * 4 + i) * 4 + j
                        there = (
                            ((z_hi + hi) % 2 * 2 + (c + core) % 2) * 16 + (z_lo + lo) % 4 * 4 + (i + x) % 4
                        ) * 4 + (j + y) % 4
                        pairs.append((here, there))
    return lax.ppermute(array, AXES, pairs)


def exchange(array, turn):
    pairs = []
    for row in range(4):
        flip = 1 if row % 2 == turn else 3
        for col in range(16):
            for y in range(4):
                pairs.append(((row * 16 + col) * 4 + y, (row * 16 + col) * 4 + (y ^ flip)))
    return lax.ppermute(array, AXES, pairs)


def after(array, *others):
    return lax.optimization_barrier((array, *others))[0]


def front(token_block, cot_block, weights):
    in_mine, in_other, out_mine, out_other = weights
    other = jnp.stack([dot(token_block, in_other, (1, 0)).astype(BF), dot(cot_block, out_other, (1, 1)).astype(BF)])
    mine = jnp.stack([dot(token_block, in_mine, (1, 0)), dot(cot_block, out_mine, (1, 1))])
    return mine + send(other, core=1).astype(F32)


def cross(total):
    payload = total.astype(BF)
    return payload, send(payload, hi=1)


def middle(total, arrived):
    both = total + arrived.astype(F32)
    value, slope = gelu_pair(both[0])
    return jnp.stack([value.astype(BF), (both[1] * slope).astype(BF)])


def back(mine, other, weights):
    in_mine, in_other, out_mine, out_other = weights
    return jnp.stack(
        [
            dot(mine[0], out_mine, (1, 0)) + dot(other[0], out_other, (1, 0)),
            dot(mine[1], in_mine, (1, 1)) + dot(other[1], in_other, (1, 1)),
        ]
    )


def local(tokens, w_in, w_out, grad_out):
    core = lax.axis_index("row") % 2
    y = lax.axis_index("depth")
    weights = lax.optimization_barrier(
        (
            lax.dynamic_slice_in_dim(w_in, core * 768, 768, axis=1),
            lax.dynamic_slice_in_dim(w_in, (1 - core) * 768, 768, axis=1),
            lax.dynamic_slice_in_dim(w_out, core * 768, 768, axis=0),
            lax.dynamic_slice_in_dim(w_out, (1 - core) * 768, 768, axis=0),
        )
    )
    first = y ^ (1 + 2 * core)
    second = y ^ (3 - 2 * core)

    own = jnp.stack([tokens, grad_out])
    block0 = jnp.concatenate([own] + [send(own, lo=-k) for k in (1, 2, 3)], axis=1)
    block1 = send(block0, x=-1)
    block3 = send(block0, x=-3)
    near = jnp.concatenate([block1, block3], axis=1)
    total0 = front(block0[0], block0[1], weights)
    payload0, arrived0 = cross(total0)
    total1 = front(near[0], near[1], weights)
    payload1, arrived1 = cross(total1)
    block1, block3 = after(block1, payload1), after(block3, payload1)
    block2 = jnp.stack([send(block1[0], x=-1), send(block3[1], x=1)])
    total2 = front(block2[0], block2[1], weights)
    payload2, arrived2 = cross(total2)

    def split(rows, shift):
        def quarter(q):
            return lax.dynamic_slice_in_dim(rows, (q + shift) % 4 * 384, 384, axis=1)

        return quarter(y), quarter(second), jnp.concatenate([quarter(first), quarter(y ^ 2)], axis=1)

    def pair_rows(mine, other):
        own, second_part, out = split(jnp.concatenate([mine[0], other[0]], axis=1), 2 * core)
        low = jnp.where(core == 0, mine[1], other[1])
        high = jnp.where(core == 0, other[1], mine[1])
        grad = jnp.concatenate([low, high], axis=1)
        return own, second_part, grad, jnp.concatenate([out, grad], axis=1)

    token0 = split(jnp.concatenate([block0[0], near[0]], axis=0), 0)
    cot0 = jnp.concatenate([block0[1], near[1]], axis=0)
    far0 = exchange(after(jnp.concatenate([cot0, token0[2]], axis=1), payload1), 0)
    token1 = split(block2[0], 0)

    mine0 = middle(total0, after(arrived0, payload2))
    other0 = send(mine0, core=1)
    pair0 = pair_rows(mine0, other0)
    far1 = exchange(jnp.concatenate([block2[1], token1[2], pair0[3]], axis=1), 0)

    mine1 = middle(total1, after(arrived1, far0))
    other1 = send(mine1, core=1)
    pair1 = pair_rows(mine1, other1)
    got1 = exchange(pair1[3], 0)
    result01 = back(
        after(jnp.concatenate([mine0, mine1], axis=1), pair1[3]), jnp.concatenate([other0, other1], axis=1), weights
    )
    result0, result1 = result01[:, :96], result01[:, 96:].astype(BF)
    mine2 = middle(total2, after(arrived2, pair1[3]))
    other2 = send(after(mine2, result1), core=1)
    pair2 = pair_rows(after(mine2, far1, far0), other2)
    got2 = exchange(pair2[3], 0)

    cot_pair = jnp.concatenate([cot0, block2[1], far0[:, :1536], far1[:, :1536]], axis=0)
    token_own = jnp.concatenate([token0[0], token1[0], far0[:, 1536:1920], far1[:, 1536:1920]], axis=0)
    token_second = jnp.concatenate([token0[1], token1[1], far0[:, 1920:], far1[:, 1920:2304]], axis=0)
    cot_pair, token_own, token_second = lax.optimization_barrier((cot_pair, token_own, token_second))

    pairs = (pair0, pair1, pair2)
    gots = (far1[:, 2304:], got1, got2)

    def joined(i, cols):
        return jnp.concatenate([p[i] for p in pairs] + [p[:, cols] for p in gots], axis=0)

    act_own = joined(0, slice(0, 384))
    act_second = joined(1, slice(384, 768))
    grad_pair = joined(2, slice(768, 2304))
    act_own, act_second, grad_pair = lax.optimization_barrier((act_own, act_second, grad_pair))
    out_sent = dot(act_second, cot_pair, (0, 0)).astype(BF)
    out_kept, in_kept = lax.optimization_barrier(
        (dot(act_own, cot_pair, (0, 0)), dot(token_own, grad_pair, (0, 0)))
    )
    in_sent = dot(after(token_second, out_kept, in_kept), grad_pair, (0, 0)).astype(BF)
    grad_w_out = (out_kept + exchange(out_sent, 1).astype(F32)).astype(BF)
    grad_w_in = (in_kept + exchange(in_sent, 1).astype(F32)).astype(BF)

    result2 = back(after(mine2, pair2[3]), other2, weights).astype(BF)
    total = result0
    for part in (send(result1[:, :96], x=1), send(result1[:, 96:], x=3), send(result2, x=2)):
        total = total + part.astype(F32)
    total = after(total, out_sent, in_sent)
    arrived = [send(total[:, 24 * k : 24 * k + 24].astype(BF), lo=k) for k in (1, 2, 3)]

    sums = total[:, :24]
    for part in arrived:
        sums = sums + after(part, grad_w_out, grad_w_in).astype(F32)
    layer_out = sums[0].astype(BF)
    grad_tokens = sums[1].astype(BF)
    return (layer_out, grad_tokens, grad_w_in, grad_w_out)


def solution(mesh):
    return jax.shard_map(
        local,
        mesh=mesh,
        in_specs=(
            P(("depth", "col"), "row"),
            P("row", "col"),
            P("col", "row"),
            P(("depth", "col"), "row"),
        ),
        out_specs=(
            P(("depth", "col"), "row"),
            P(("depth", "col"), "row"),
            P(("row", "depth"), "col"),
            P(("col", "depth"), "row"),
        ),
        check_vma=False,
    )
```

```python
import jax
import jax.numpy as jnp
from jax import lax
from jax.sharding import PartitionSpec as P

coef = 0.7978845608
AXES = ("row", "col", "depth")
BF = jnp.bfloat16
F32 = jnp.float32


def gelu_pair(z):
    t = jnp.tanh(coef * (z + 0.044715 * z * z * z))
    value = 0.5 * z * (1.0 + t)
    slope = 0.5 * (1.0 + t) + 0.5 * z * (1.0 - t * t) * coef * (1.0 + 0.134145 * z * z)
    return (value, slope)


def dot(left, right, dims):
    return lax.dot_general(left, right, ((dims[:1], dims[1:]), ((), ())), preferred_element_type=F32)


def send(array, hi=0, core=0, lo=0, x=0, y=0):
    pairs = []
    for z_hi in range(2):
        for c in range(2):
            for z_lo in range(4):
                for i in range(4):
                    for j in range(4):
                        here = ((z_hi * 2 + c) * 16 + z_lo * 4 + i) * 4 + j
                        there = (
                            ((z_hi + hi) % 2 * 2 + (c + core) % 2) * 16 + (z_lo + lo) % 4 * 4 + (i + x) % 4
                        ) * 4 + (j + y) % 4
                        pairs.append((here, there))
    return lax.ppermute(array, AXES, pairs)


def exchange(array, turn):
    pairs = []
    for row in range(4):
        flip = 1 if row % 2 == turn else 3
        for col in range(16):
            for y in range(4):
                pairs.append(((row * 16 + col) * 4 + y, (row * 16 + col) * 4 + (y ^ flip)))
    return lax.ppermute(array, AXES, pairs)


def after(array, *others):
    return lax.optimization_barrier((array, *others))[0]


def front(token_block, cot_block, weights):
    in_mine, in_other, out_mine, out_other = weights
    other = jnp.stack([dot(token_block, in_other, (1, 0)).astype(BF), dot(cot_block, out_other, (1, 1)).astype(BF)])
    mine = jnp.stack([dot(token_block, in_mine, (1, 0)), dot(cot_block, out_mine, (1, 1))])
    return mine + send(other, core=1).astype(F32)


def cross(total):
    payload = total.astype(BF)
    return payload, send(payload, hi=1)


def middle(total, arrived):
    both = total + arrived.astype(F32)
    value, slope = gelu_pair(both[0])
    return jnp.stack([value.astype(BF), (both[1] * slope).astype(BF)])


def back(mine, other, weights):
    in_mine, in_other, out_mine, out_other = weights
    return jnp.stack(
        [
            dot(mine[0], out_mine, (1, 0)) + dot(other[0], out_other, (1, 0)),
            dot(mine[1], in_mine, (1, 1)) + dot(other[1], in_other, (1, 1)),
        ]
    )


def local(tokens, w_in, w_out, grad_out):
    core = lax.axis_index("row") % 2
    y = lax.axis_index("depth")
    weights = lax.optimization_barrier(
        (
            lax.dynamic_slice_in_dim(w_in, core * 768, 768, axis=1),
            lax.dynamic_slice_in_dim(w_in, (1 - core) * 768, 768, axis=1),
            lax.dynamic_slice_in_dim(w_out, core * 768, 768, axis=0),
            lax.dynamic_slice_in_dim(w_out, (1 - core) * 768, 768, axis=0),
        )
    )
    first = y ^ (1 + 2 * core)
    second = y ^ (3 - 2 * core)

    own = jnp.stack([tokens, grad_out])
    block0 = jnp.concatenate([own] + [send(own, lo=-k) for k in (1, 2, 3)], axis=1)
    block1 = send(block0, x=-1)
    block3 = send(block0, x=-3)
    near = jnp.concatenate([block1, block3], axis=1)
    total0 = front(block0[0], block0[1], weights)
    payload0, arrived0 = cross(total0)
    total1 = front(near[0], near[1], weights)
    payload1, arrived1 = cross(total1)
    block1, block3 = after(block1, payload1), after(block3, payload1)
    block2 = jnp.stack([send(block1[0], x=-1), send(block3[1], x=1)])
    total2 = front(block2[0], block2[1], weights)
    payload2 = total2.astype(BF)

    def split(rows, shift):
        def quarter(q):
            return lax.dynamic_slice_in_dim(rows, (q + shift) % 4 * 384, 384, axis=1)

        return quarter(y), quarter(second), jnp.concatenate([quarter(first), quarter(y ^ 2)], axis=1)

    def pair_rows(mine, other):
        own, second_part, out = split(jnp.concatenate([mine[0], other[0]], axis=1), 2 * core)
        low = jnp.where(core == 0, mine[1], other[1])
        high = jnp.where(core == 0, other[1], mine[1])
        grad = jnp.concatenate([low, high], axis=1)
        return own, second_part, grad, jnp.concatenate([out, grad], axis=1)

    token0 = split(jnp.concatenate([block0[0], near[0]], axis=0), 0)
    cot0 = jnp.concatenate([block0[1], near[1]], axis=0)
    far0 = exchange(after(jnp.concatenate([cot0, token0[2]], axis=1), payload1), 0)
    token1 = split(block2[0], 0)

    mine0 = middle(total0, after(arrived0, payload2))
    other0 = send(mine0, core=1)
    pair0 = pair_rows(mine0, other0)
    arrived2 = send(after(payload2, other0), hi=1)
    far1 = exchange(jnp.concatenate([block2[1], token1[2], pair0[3]], axis=1), 0)

    mine1 = middle(total1, after(arrived1, far0))
    other1 = send(mine1, core=1)
    pair1 = pair_rows(mine1, other1)
    got1 = exchange(pair1[3], 0)
    result01 = back(
        after(jnp.concatenate([mine0, mine1], axis=1), pair1[3]), jnp.concatenate([other0, other1], axis=1), weights
    )
    result0, result1 = result01[:, :96], result01[:, 96:].astype(BF)
    mine2 = middle(total2, after(arrived2, pair1[3]))
    other2 = send(after(mine2, result1), core=1)
    pair2 = pair_rows(after(mine2, far1, far0), other2)
    got2 = exchange(pair2[3], 0)

    cot_pair = jnp.concatenate([cot0, block2[1], far0[:, :1536], far1[:, :1536]], axis=0)
    token_own = jnp.concatenate([token0[0], token1[0], far0[:, 1536:1920], far1[:, 1536:1920]], axis=0)
    token_second = jnp.concatenate([token0[1], token1[1], far0[:, 1920:], far1[:, 1920:2304]], axis=0)
    cot_pair, token_own, token_second = lax.optimization_barrier((cot_pair, token_own, token_second))

    pairs = (pair0, pair1, pair2)
    gots = (far1[:, 2304:], got1, got2)

    def joined(i, cols):
        return jnp.concatenate([p[i] for p in pairs] + [p[:, cols] for p in gots], axis=0)

    act_own = joined(0, slice(0, 384))
    act_second = joined(1, slice(384, 768))
    grad_pair = joined(2, slice(768, 2304))
    act_own, act_second, grad_pair = lax.optimization_barrier((act_own, act_second, grad_pair))
    out_sent = dot(act_second, cot_pair, (0, 0)).astype(BF)
    out_kept, in_kept = lax.optimization_barrier(
        (dot(act_own, cot_pair, (0, 0)), dot(token_own, grad_pair, (0, 0)))
    )
    in_sent = dot(after(token_second, out_kept, in_kept), grad_pair, (0, 0)).astype(BF)
    grad_w_out = (out_kept + exchange(out_sent, 1).astype(F32)).astype(BF)
    grad_w_in = (in_kept + exchange(in_sent, 1).astype(F32)).astype(BF)

    result2 = back(after(mine2, pair2[3]), other2, weights).astype(BF)
    total = result0
    for part in (send(result1[:, :96], x=1), send(result1[:, 96:], x=3), send(result2, x=2)):
        total = total + part.astype(F32)
    total = after(total, out_sent, in_sent)
    arrived = [send(total[:, 24 * k : 24 * k + 24].astype(BF), lo=k) for k in (1, 2, 3)]

    layer_sum, token_sum = total[0, :24], total[1, :24]
    for part in arrived:
        part = after(part, grad_w_out, grad_w_in).astype(F32)
        layer_sum, token_sum = layer_sum + part[0], token_sum + part[1]
    layer_out, grad_tokens = layer_sum.astype(BF), token_sum.astype(BF)
    return (layer_out, grad_tokens, grad_w_in, grad_w_out)


def solution(mesh):
    return jax.shard_map(
        local,
        mesh=mesh,
        in_specs=(
            P(("depth", "col"), "row"),
            P("row", "col"),
            P("col", "row"),
            P(("depth", "col"), "row"),
        ),
        out_specs=(
            P(("depth", "col"), "row"),
            P(("depth", "col"), "row"),
            P(("row", "depth"), "col"),
            P(("col", "depth"), "row"),
        ),
        check_vma=False,
    )
```
